32 devices in a mesh: group: 2 (over x), dx: 16 (over z, y, core).
Axes of the slice: x: 2, y: 2, z: 4, core: 2. Of those that a mesh axis runs over, the one named last changes fastest.
Arguments:
- points: bfloat16 [16384, 1024], P(('group', 'dx')), parts along dimension 0, may hold values from -6 to 6
- cotangent: bfloat16 [16384, 1024], P(('group', 'dx')), parts along dimension 0, may hold values from -96 to 96
- counts: int32 [32], P(('group', 'dx')), parts along dimension 0, may hold values from 170 to 512, as said below
- w_query: bfloat16 [1024, 1024], replicated, may hold values from -0.1875 to 0.1875
- w_key: bfloat16 [1024, 1024], replicated, may hold values from -0.1875 to 0.1875
- w_value: bfloat16 [1024, 1024], replicated, may hold values from -0.1875 to 0.1875
- gain_key: float32 [1024], replicated, may hold values from 0.25 to 1.75
- bias_key: float32 [1024], replicated, may hold values from -3 to 3
- gain_value: float32 [1024], replicated, may hold values from 0.25 to 1.75
- bias_value: float32 [1024], replicated, may hold values from -3 to 3
Outputs:
- grad_points: bfloat16 [16384, 1024], P(('group', 'dx')), parts along dimension 0
The draws below stay inside these ranges and needn't reach their ends.
There are 2 independent parts, one for each index of `group`. The reference program is written for one: setup_inputs(seed, part) draws one part's arguments, and reference() takes and returns one part's arrays. A program takes and returns all parts, laid end to end along the dimension named above; an argument that names none is the same for every part. Nothing has to cross between parts.
Inputs may be any that keep to these rules, and one draw needn't show every extreme that they name: `counts`: live points of each tile; some tile of every slab holds 512.
All inputs are finite; a program needn't handle non-finite values.
Results may differ from the reference program's by a relative error of at most 0.006.
Values sent between devices are 32-bit elements; how exact they have to be, the bound alone decides.
A program may use at most 64 MiB of HBM per device.

```python
import jax
import jax.numpy as jnp
from jax import lax

D = 1024
HEADS = 8
CAP = 512
NTILES = 16
NPTS = 8192


def draw_counts(key, part):
    first_key = jax.random.fold_in(key, 11)
    second_key = jax.random.fold_in(key, 23)
    steps = jnp.arange(NTILES, dtype=jnp.int32)
    spread = 2 * CAP // 3 - CAP // 8
    ramp = CAP // 3 + spread * steps // max(NTILES - 1, 1)
    jitter = jax.random.randint(first_key, (NTILES,), 0, CAP // 8 + 1)
    filled = jnp.minimum(ramp + jitter, CAP)
    chosen = jax.random.randint(second_key, (), 3 * NTILES // 4, NTILES)
    return jnp.where(steps == chosen, CAP, filled).astype(jnp.int32)


def steps_of(rng, dims, split, smallest, top_value):
    factor_of, own = 1.0, jax.random.fold_in(rng, 6)
    for dim, blocks in split:
        steps = jnp.exp(jax.random.uniform(jax.random.fold_in(own, dim), (blocks,), jnp.float32, smallest / len(split), top_value / len(split)))
        factor_of = factor_of * jnp.repeat(steps, dims[dim] // blocks).reshape([-1 if axis == dim else 1 for axis in range(len(dims))])
    return factor_of


def gaussian(rng, shape, deviation, reach, pieces=(), kind=jnp.bfloat16):
    loudness = steps_of(rng, shape, pieces, -0.22, 0.18) if pieces else 1.0
    result = jax.random.normal(rng, shape, jnp.float32) * deviation * loudness
    return jnp.minimum(jnp.maximum(result, -reach), reach).astype(kind)


def setup_inputs(seed: int = 0, part: int = 0) -> dict:
    seeds = jax.random.split(jax.random.key(seed), 11)
    own_keys = jax.random.split(jax.random.fold_in(seeds[10], part), 11)
    points = gaussian(own_keys[0], (NPTS, D), 1.0, 6.0, ((0, 16),))
    cotangent = gaussian(own_keys[1], (NPTS, D), 16.0, 96.0, ((0, 16),))
    counts = draw_counts(jax.random.fold_in(jax.random.fold_in(seeds[10], part), 71), part)
    w_query = gaussian(seeds[3], (D, D), D ** -0.5, 0.1875)
    w_key = gaussian(seeds[4], (D, D), D ** -0.5, 0.1875)
    w_value = gaussian(seeds[5], (D, D), D ** -0.5, 0.1875)
    gain_key = jnp.clip(1.0 + 0.15 * jax.random.normal(seeds[6], (D,), jnp.float32), 0.25, 1.75)
    bias_key = gaussian(seeds[7], (D,), 0.5, 3.0, (), jnp.float32)
    gain_value = jnp.clip(1.0 + 0.15 * jax.random.normal(seeds[8], (D,), jnp.float32), 0.25, 1.75)
    bias_value = gaussian(seeds[9], (D,), 0.5, 3.0, (), jnp.float32)
    return {"points": points, "cotangent": cotangent, "counts": counts, "w_query": w_query, "w_key": w_key, "w_value": w_value, "gain_key": gain_key, "bias_key": bias_key, "gain_value": gain_value, "bias_value": bias_value}


eps = 1e-05

def head_norm(raw):
    grouped = raw.reshape(raw.shape[0], HEADS, -1)
    center = grouped - lax.optimization_barrier(jnp.mean(grouped, axis=2, keepdims=True))
    inverse = lax.rsqrt(lax.optimization_barrier(jnp.mean(center * center, axis=2, keepdims=True)) + eps)
    return (center * inverse, inverse)

def norm_back(grad, gain, normed, inverse):
    scaled = grad * gain.reshape(HEADS, -1)
    inner = scaled - lax.optimization_barrier(jnp.mean(scaled, axis=2, keepdims=True))
    inner = inner - normed * lax.optimization_barrier(jnp.mean(scaled * normed, axis=2, keepdims=True))
    return (inverse * inner).reshape(grad.shape[0], -1).astype(jnp.bfloat16)

def reference(points, cotangent, counts, w_query, w_key, w_value, gain_key, bias_key, gain_value, bias_value):
    slot = jnp.arange(NPTS, dtype=jnp.int32)
    live = (slot % CAP < jnp.repeat(counts, CAP)).astype(jnp.float32)[:, None]
    total = jnp.sum(counts).astype(jnp.float32)
    query = jnp.dot(points, w_query, preferred_element_type=jnp.float32).astype(jnp.bfloat16)
    key_hat, key_inv = head_norm(jnp.dot(points, w_key, preferred_element_type=jnp.float32))
    value_hat, value_inv = head_norm(jnp.dot(points, w_value, preferred_element_type=jnp.float32))
    live_h = live[:, :, None]
    keys = (live_h * (key_hat * gain_key.reshape(HEADS, -1) + bias_key.reshape(HEADS, -1))).astype(jnp.bfloat16)
    values = (live_h * (value_hat * gain_value.reshape(HEADS, -1) + bias_value.reshape(HEADS, -1))).astype(jnp.bfloat16)
    cot = cotangent.reshape(NPTS, HEADS, -1).astype(jnp.float32)
    masked_query = (query.astype(jnp.float32) * live).reshape(NPTS, HEADS, -1)
    gram = (jnp.einsum('nhi,nhj->hij', keys.astype(jnp.float32), values.astype(jnp.float32)) / total).astype(jnp.bfloat16)
    dgram = (jnp.einsum('nhi,nhj->hij', masked_query, cot) / total).astype(jnp.bfloat16)
    dquery = (live_h * jnp.einsum('nhj,hij->nhi', cot, gram.astype(jnp.float32))).reshape(NPTS, D).astype(jnp.bfloat16)
    dkeys = jnp.einsum('nhj,hij->nhi', values.astype(jnp.float32), dgram.astype(jnp.float32))
    dvalues = jnp.einsum('nhi,hij->nhj', keys.astype(jnp.float32), dgram.astype(jnp.float32))
    dkey_raw = norm_back(dkeys, gain_key, key_hat, key_inv)
    dvalue_raw = norm_back(dvalues, gain_value, value_hat, value_inv)
    grad = jnp.dot(dquery, w_query.T, preferred_element_type=jnp.float32)
    grad = grad + jnp.dot(dkey_raw, w_key.T, preferred_element_type=jnp.float32)
    grad = grad + jnp.dot(dvalue_raw, w_value.T, preferred_element_type=jnp.float32)
    return grad.astype(jnp.bfloat16)
```

```python
import functools

import jax
import jax.numpy as jnp
from jax import lax
from jax.experimental import pallas as pl
from jax.experimental.pallas import tpu as pltpu
from jax.sharding import PartitionSpec as P

HEADS = 8
EPS = 1e-05
MESH = pl.DeviceIdType.MESH
F32 = jnp.float32
BF16 = jnp.bfloat16
NT = (((1,), (1,)), ((), ()))
TN = (((0,), (0,)), ((), ()))
NN = (((1,), (0,)), ((), ()))


def mm(a, b, dims):
    return lax.dot_general(a, b, dims, preferred_element_type=F32)


def kernel(
    n,
    counts,
    points_hbm,
    cot_hbm,
    wq_hbm,
    wk_hbm,
    wv_hbm,
    gain_k,
    bias_k,
    gain_v,
    bias_v,
    out_hbm,
    points,
    cot,
    wq,
    wk,
    wv,
    khat,
    vhat,
    kinv,
    vinv,
    keys,
    values,
    dq,
    dk,
    dv,
    acc,
    out,
    loc,
    r1,
    p1,
    r2,
    p2,
    r3,
    p3,
    full,
    cnt,
    cr,
    load_sem,
    store_sem,
    send_sem,
    recv_sem,
    csend_sem,
    crecv_sem,
):
    rows, width = points.shape
    hd = width // HEADS
    pair = 2 * hd
    npair = HEADS // 2
    grows = HEADS * hd
    far = n // 4
    piece = grows // n

    me = lax.axis_index("dx")
    core = lax.rem(me, 2)
    mid = lax.rem(me // 2, 2)
    hi = me // 4
    core_peer = me + 1 - 2 * core
    mid_peer = me + 2 - 4 * mid
    low = lax.rem(me, 4)
    far_peers = [lax.rem(hi + d, far) * 4 + low for d in range(1, far)]

    def load(src, dst, i):
        return pltpu.make_async_copy(src, dst, load_sem.at[i])

    loads = [
        load(points_hbm, points, 0),
        load(wq_hbm, wq, 1),
        load(cot_hbm, cot, 2),
        load(wk_hbm, wk, 3),
        load(wv_hbm, wv, 4),
    ]
    for c in loads:
        c.start()

    barrier = pltpu.get_barrier_semaphore()
    for p in [core_peer, mid_peer] + far_peers:
        pl.semaphore_signal(barrier, inc=1, device_id={"dx": p}, device_id_type=MESH)

    own_count = counts[0]

    def live(cols):
        return lax.broadcasted_iota(jnp.int32, (rows, cols), 0) < own_count

    def rcopy(src, dst, sems, rsems, k, peer):
        return pltpu.make_async_remote_copy(
            src_ref=src,
            dst_ref=dst,
            send_sem=sems.at[k],
            recv_sem=rsems.at[k],
            device_id={"dx": peer},
            device_id_type=MESH,
        )

    half, quarter = grows // 2, grows // 4

    def block(i, size):
        return pl.ds(pl.multiple_of(i * size, size), size)

    sent = []

    def go(copies):
        for c in copies:
            c.start()
        sent.extend(copies)

    def arrive(copies):
        for c in copies:
            c.wait_recv()

    def scatter1(c):
        x = [rcopy(loc.at[c, block(1 - core, half)], r1.at[c], send_sem.at[c], recv_sem.at[c], 0, core_peer)]
        if c == 0:
            x.append(rcopy(cnt.at[0], cr.at[0], csend_sem, crecv_sem, 0, core_peer))
        go(x)
        return x

    def scatter2(c, before):
        arrive(before)
        p1[c] = loc[c, block(core, half), :] + r1[c]
        x = [rcopy(p1.at[c, block(1 - mid, quarter)], r2.at[c], send_sem.at[c], recv_sem.at[c], 1, mid_peer)]
        if c == 0:
            cnt[1] = cnt[0] + cr[0]
            x.append(rcopy(cnt.at[1], cr.at[1], csend_sem, crecv_sem, 1, mid_peer))
        go(x)
        return x

    def scatter3(c, before):
        arrive(before)
        p2[c] = p1[c, block(mid, quarter), :] + r2[c]
        x = []
        if c == 0:
            cnt[2] = cnt[1] + cr[1]
        for d in range(1, far):
            to = lax.rem(hi + d, far)
            x.append(
                rcopy(
                    p2.at[c, block(to, piece)],
                    r3.at[c, d],
                    send_sem.at[c],
                    recv_sem.at[c],
                    1 + d,
                    far_peers[d - 1],
                )
            )
            if c == 0:
                x.append(rcopy(cnt.at[2], cr.at[1 + d], csend_sem, crecv_sem, 1 + d, far_peers[d - 1]))
        go(x)
        return x

    base = far + 1
    own = core * half + mid * quarter + hi * piece

    def gather1(c, before):
        arrive(before)
        total = p2[c, block(hi, piece), :]
        for d in range(1, far):
            total = total + r3[c, d]
        if c == 0:
            people = cnt[2]
            for d in range(1, far):
                people = people + cr[1 + d]
            cnt[3] = people
        total = total / cnt[3, 0:1, :]
        where = pl.ds(pl.multiple_of(own, piece), piece)
        full[c, where, :] = total
        x = []
        for d in range(1, far):
            x.append(
                rcopy(
                    full.at[c, where],
                    full.at[c, where],
                    send_sem.at[c],
                    recv_sem.at[c],
                    base + d - 1,
                    far_peers[d - 1],
                )
            )
        go(x)
        return x

    def gather2(c, before):
        arrive(before)
        where = pl.ds(pl.multiple_of(core * half + mid * quarter, quarter), quarter)
        x = [rcopy(full.at[c, where], full.at[c, where], send_sem.at[c], recv_sem.at[c], base + far - 1, mid_peer)]
        go(x)
        return x

    def gather3(c, before):
        arrive(before)
        where = block(core, half)
        x = [rcopy(full.at[c, where], full.at[c, where], send_sem.at[c], recv_sem.at[c], base + far, core_peer)]
        go(x)
        return x

    cnt[0] = jnp.broadcast_to(own_count.astype(F32), cnt.shape[1:])
    loads[0].wait()
    loads[1].wait()
    loads[2].wait()

    @pl.loop(0, npair)
    def _(hp):
        cols = block(hp, pair)
        q = mm(points[...], wq[:, cols], NN)
        q = jnp.where(live(pair), q, 0.0).astype(BF16)
        g = mm(q, cot[:, cols], TN)
        r = pl.multiple_of(hp * pair, pair)
        loc[0, pl.ds(r, hd), :] = g[:hd, :hd]
        loc[0, pl.ds(r + hd, hd), :] = g[hd:, hd:]

    pl.semaphore_wait(barrier, far + 1)
    stage = scatter1(0)
    loads[3].wait()
    loads[4].wait()

    def norm(raw, gain, bias, hat_ref, inv_ref, dst, c0):
        for j in range(2):
            x = raw[:, j * hd : (j + 1) * hd]
            cs = slice(c0 + j * hd, c0 + (j + 1) * hd)
            center = x - jnp.mean(x, axis=1, keepdims=True)
            inv = lax.rsqrt(jnp.mean(center * center, axis=1, keepdims=True) + EPS)
            hat = center * inv
            hat_ref[:, cs] = hat
            inv_ref[:, cs] = jnp.broadcast_to(inv, hat.shape)
            y = hat * gain[:, cs] + bias[:, cs]
            dst[:, cs] = jnp.where(live(hd), y, 0.0).astype(BF16)

    def forward(hp):
        c0 = hp * pair
        cs = slice(c0, c0 + pair)
        norm(mm(points[...], wk[:, cs], NN), gain_k, bias_k, khat, kinv, keys, c0)
        norm(mm(points[...], wv[:, cs], NN), gain_v, bias_v, vhat, vinv, values, c0)
        g = mm(keys[:, cs], values[:, cs], TN)
        loc[1, c0 : c0 + hd, :] = g[:hd, :hd]
        loc[1, c0 + hd : c0 + pair, :] = g[hd:, hd:]

    steps = [scatter2, scatter3, gather1, gather2]
    for hp in range(npair):
        forward(hp)
        if hp < len(steps):
            stage = steps[hp](0, stage)

    kv = scatter1(1)
    stage = gather3(0, stage)
    kv = scatter2(1, kv)
    arrive(stage)

    def back(grad, gain, hat_ref, inv_ref, dst, cs):
        g = grad * gain[:, cs]
        hat = hat_ref[:, cs]
        inner = g - jnp.mean(g, axis=1, keepdims=True)
        inner = inner - hat * jnp.mean(g * hat, axis=1, keepdims=True)
        dst[:, cs] = (inv_ref[:, cs] * inner).astype(BF16)

    def backward(hp):
        for h in (2 * hp, 2 * hp + 1):
            cs = slice(h * hd, (h + 1) * hd)
            d = full[0, cs, :].astype(BF16)
            back(mm(values[:, cs], d, NT), gain_k, khat, kinv, dk, cs)
            back(mm(keys[:, cs], d, NN), gain_v, vhat, vinv, dv, cs)

    for hp in range(npair):
        backward(hp)
        if hp == 0:
            kv = scatter3(1, kv)
        if hp == 2:
            kv = gather1(1, kv)

    def tail(i):
        rs = block(i, pair)
        acc[:, rs] = mm(dk[...], wk[rs, :], NT) + mm(dv[...], wv[rs, :], NT)

    for i in range(npair):
        tail(i)
        if i == 0:
            kv = gather2(1, kv)
        if i == 2:
            kv = gather3(1, kv)
    arrive(kv)

    for h in range(HEADS):
        cs = slice(h * hd, (h + 1) * hd)
        g = full[1, cs, :].astype(BF16)
        dq[:, cs] = jnp.where(live(hd), mm(cot[:, cs], g, NT), 0.0).astype(BF16)

    writes = []
    for i in range(npair):
        cs = slice(i * pair, (i + 1) * pair)
        out[:, cs] = (acc[:, cs] + mm(dq[...], wq[cs, :], NT)).astype(BF16)
        w = pltpu.make_async_copy(out.at[:, cs], out_hbm.at[:, cs], store_sem.at[i])
        w.start()
        writes.append(w)
    for c in sent:
        c.wait_send()
    for w in writes:
        w.wait()


def body(n, points, cotangent, counts, w_query, w_key, w_value, gain_key, bias_key, gain_value, bias_value):
    rows, width = points.shape
    hd = width // HEADS
    grows = HEADS * hd
    far = n // 4
    piece = grows // n
    ncopies = 2 * (far + 1)
    anyspec = pl.BlockSpec(memory_space=pl.ANY)
    vspec = pl.BlockSpec(memory_space=pltpu.VMEM)

    def v(shape, dtype):
        return pltpu.VMEM(shape, dtype)

    return pl.pallas_call(
        functools.partial(kernel, n),
        out_shape=jax.ShapeDtypeStruct((rows, width), BF16),
        in_specs=[pl.BlockSpec(memory_space=pltpu.SMEM)] + [anyspec] * 5 + [vspec] * 4,
        out_specs=anyspec,
        scratch_shapes=[
            v((rows, width), BF16),
            v((rows, width), BF16),
            v((width, width), BF16),
            v((width, width), BF16),
            v((width, width), BF16),
            v((rows, width), F32),
            v((rows, width), F32),
            v((rows, width), F32),
            v((rows, width), F32),
            v((rows, width), BF16),
            v((rows, width), BF16),
            v((rows, width), BF16),
            v((rows, width), BF16),
            v((rows, width), BF16),
            v((rows, width), F32),
            v((rows, width), BF16),
            v((2, grows, hd), F32),
            v((2, grows // 2, hd), F32),
            v((2, grows // 2, hd), F32),
            v((2, grows // 4, hd), F32),
            v((2, grows // 4, hd), F32),
            v((2, far, piece, hd), F32),
            v((2, piece, hd), F32),
            v((2, grows, hd), F32),
            v((4, 8, hd), F32),
            v((far + 1, 8, hd), F32),
            pltpu.SemaphoreType.DMA((5,)),
            pltpu.SemaphoreType.DMA((HEADS // 2,)),
            pltpu.SemaphoreType.DMA((2, ncopies)),
            pltpu.SemaphoreType.DMA((2, ncopies)),
            pltpu.SemaphoreType.DMA((far + 1,)),
            pltpu.SemaphoreType.DMA((far + 1,)),
        ],
        compiler_params=pltpu.CompilerParams(
            collective_id=0, has_side_effects=True, vmem_limit_bytes=52 * 2**20
        ),
        cost_estimate=pl.CostEstimate(
            flops=12 * rows * width * width, bytes_accessed=12 * 2**20, transcendentals=0
        ),
    )(
        counts,
        points,
        cotangent,
        w_query,
        w_key,
        w_value,
        gain_key.reshape(1, -1),
        bias_key.reshape(1, -1),
        gain_value.reshape(1, -1),
        bias_value.reshape(1, -1),
    )


def solution(mesh):
    split = P(("group", "dx"), None)
    placed = (split, split, P(("group", "dx")), P(), P(), P(), P(), P(), P(), P())
    return jax.shard_map(
        functools.partial(body, mesh.shape["dx"]),
        mesh=mesh,
        in_specs=placed,
        out_specs=split,
        check_vma=False,
    )
```

```python
import functools

import jax
import jax.numpy as jnp
from jax import lax
from jax.experimental import pallas as pl
from jax.experimental.pallas import tpu as pltpu
from jax.sharding import PartitionSpec as P

HEADS = 8
EPS = 1e-05
MESH = pl.DeviceIdType.MESH
F32 = jnp.float32
BF16 = jnp.bfloat16
NT = (((1,), (1,)), ((), ()))
TN = (((0,), (0,)), ((), ()))
NN = (((1,), (0,)), ((), ()))


def mm(a, b, dims):
    return lax.dot_general(a, b, dims, preferred_element_type=F32)


def kernel(
    n,
    counts,
    points_hbm,
    cot_hbm,
    wq_hbm,
    wk_hbm,
    wv_hbm,
    gk_hbm,
    bk_hbm,
    gv_hbm,
    bv_hbm,
    out,
    points,
    cot,
    wq,
    wk,
    wv,
    khat,
    vhat,
    kinv,
    vinv,
    keys,
    values,
    dq,
    dk,
    dv,
    gain_k,
    bias_k,
    gain_v,
    bias_v,
    acc,
    loc,
    r1,
    p1,
    r3,
    full,
    cnt,
    load_sem,
    send_sem,
    recv_sem,
    csend_sem,
    crecv_sem,
):
    rows, width = points.shape
    hd = width // HEADS
    pair = 2 * hd
    npair = HEADS // 2
    grows = HEADS * hd
    chips = n // 2
    piece = grows // n

    me = lax.axis_index("dx")
    core = lax.rem(me, 2)
    chip = me // 2
    core_peer = me + 1 - 2 * core
    chip_peers = [lax.rem(chip + d, chips) * 2 + core for d in range(1, chips)]

    def load(src, dst, i):
        return pltpu.make_async_copy(src, dst, load_sem.at[i])

    loads = [
        load(points_hbm, points, 0),
        load(wq_hbm, wq, 1),
        load(cot_hbm, cot, 2),
        load(wk_hbm, wk, 3),
        load(wv_hbm, wv, 4),
        load(gk_hbm, gain_k, 5),
        load(bk_hbm, bias_k, 6),
        load(gv_hbm, gain_v, 7),
        load(bv_hbm, bias_v, 8),
    ]
    for c in loads:
        c.start()

    barrier = pltpu.get_barrier_semaphore()
    for p in [core_peer] + chip_peers:
        pl.semaphore_signal(barrier, inc=1, device_id={"dx": p}, device_id_type=MESH)

    own_count = counts[0]

    def live(cols):
        return lax.broadcasted_iota(jnp.int32, (rows, cols), 0) < own_count

    def rcopy(src, dst, sems, rsems, k, peer):
        return pltpu.make_async_remote_copy(
            src_ref=src,
            dst_ref=dst,
            send_sem=sems.at[k],
            recv_sem=rsems.at[k],
            device_id={"dx": peer},
            device_id_type=MESH,
        )

    half = grows // 2

    def block(i, size):
        return pl.ds(pl.multiple_of(i * size, size), size)

    sent = []

    def go(copies):
        for c in copies:
            c.start()
        sent.extend(copies)

    def arrive(copies):
        for c in copies:
            c.wait_recv()

    def core_scatter(c):
        x = [rcopy(loc.at[c, block(1 - core, half)], r1.at[c], send_sem.at[c], recv_sem.at[c], 0, core_peer)]
        if c == 0:
            x.append(rcopy(cnt.at[0], cnt.at[1], csend_sem, crecv_sem, 0, core_peer))
        go(x)
        return x

    def chip_scatter(c, before):
        arrive(before)
        for j in range(chips):
            mine = pl.ds(pl.multiple_of(core * half + j * piece, piece), piece)
            p1[c, j, 0:piece, :] = loc[c, mine, :] + r1[c, j * piece : (j + 1) * piece, :]
        if c == 0:
            people = cnt[0] + cnt[1]
            for j in range(chips):
                p1[c, j, piece:, :] = people
        size = piece + 8 if c == 0 else piece
        x = []
        for d in range(1, chips):
            x.append(
                rcopy(
                    p1.at[c, lax.rem(chip + d, chips), pl.ds(0, size)],
                    r3.at[c, d, pl.ds(0, size)],
                    send_sem.at[c],
                    recv_sem.at[c],
                    d,
                    chip_peers[d - 1],
                )
            )
        go(x)
        return x

    def span(j):
        return pl.ds(pl.multiple_of(core * half + j * piece, piece), piece)

    def chip_gather(c, before):
        arrive(before)
        total = p1[c, chip, 0:piece, :]
        for d in range(1, chips):
            total = total + r3[c, d, 0:piece, :]
        if c == 0:
            people = p1[c, chip, piece:, :]
            for d in range(1, chips):
                people = people + r3[c, d, piece:, :]
            cnt[2] = people
        full[c, span(chip), :] = total / cnt[2, 0:1, :]
        x = []
        for d in range(1, chips):
            x.append(
                rcopy(
                    full.at[c, span(chip)],
                    full.at[c, span(chip)],
                    send_sem.at[c],
                    recv_sem.at[c],
                    chips + d,
                    chip_peers[d - 1],
                )
            )
        go(x)
        y = [core_forward(c, 0)]
        go(y)
        return x, y

    def core_forward(c, d):
        rs = span(lax.rem(chip + chips - d, chips))
        return rcopy(full.at[c, rs], full.at[c, rs], send_sem.at[c], recv_sem.at[c], 2 * chips + d, core_peer)

    def core_gather(c, before):
        x, y = before
        for d in range(1, chips):
            x[d - 1].wait_recv()
            f = core_forward(c, d)
            go([f])
            y.append(f)
        return y

    own_pairs = [core * (npair // 2) + i for i in range(npair // 2)]
    peer_pairs = [(1 - core) * (npair // 2) + i for i in range(npair // 2)]

    cnt[0] = jnp.broadcast_to(own_count.astype(F32), cnt.shape[1:])
    loads[0].wait()
    loads[1].wait()
    loads[2].wait()

    def query(hp):
        cols = block(hp, pair)
        q = mm(points[...], wq[:, cols], NN)
        q = jnp.where(live(pair), q, 0.0).astype(BF16)
        g = mm(q, cot[:, cols], TN)
        r = pl.multiple_of(hp * pair, pair)
        loc[0, pl.ds(r, hd), :] = g[:hd, :hd]
        loc[0, pl.ds(r + hd, hd), :] = g[hd:, hd:]

    for hp in peer_pairs:
        query(hp)
    pl.semaphore_wait(barrier, chips)
    qdy = core_scatter(0)
    for hp in own_pairs:
        query(hp)
    for c in loads[3:]:
        c.wait()
    qdy = chip_scatter(0, qdy)

    def norm(raw, gain, bias, hat_ref, inv_ref, dst, c0):
        for j in range(2):
            x = raw[:, j * hd : (j + 1) * hd]
            cs = pl.ds(pl.multiple_of(c0 + j * hd, hd), hd)
            center = x - jnp.mean(x, axis=1, keepdims=True)
            inv = lax.rsqrt(jnp.mean(center * center, axis=1, keepdims=True) + EPS)
            hat = center * inv
            hat_ref[:, cs] = hat
            inv_ref[:, cs] = jnp.broadcast_to(inv, hat.shape)
            y = hat * gain[:, cs] + bias[:, cs]
            dst[:, cs] = jnp.where(live(hd), y, 0.0).astype(BF16)

    def forward(hp):
        c0 = pl.multiple_of(hp * pair, pair)
        cs = pl.ds(c0, pair)
        norm(mm(points[...], wk[:, cs], NN), gain_k, bias_k, khat, kinv, keys, c0)
        norm(mm(points[...], wv[:, cs], NN), gain_v, bias_v, vhat, vinv, values, c0)
        g = mm(keys[:, cs], values[:, cs], TN)
        loc[1, pl.ds(c0, hd), :] = g[:hd, :hd]
        loc[1, pl.ds(pl.multiple_of(c0 + hd, hd), hd), :] = g[hd:, hd:]

    for hp in peer_pairs:
        forward(hp)
    kv = core_scatter(1)
    for hp in own_pairs:
        forward(hp)
    kv = chip_scatter(1, kv)
    qdy = chip_gather(0, qdy)
    kv = chip_gather(1, kv)
    qdy = core_gather(0, qdy)

    def back(grad, gain, hat_ref, inv_ref, dst, cs):
        g = grad * gain[:, cs]
        hat = hat_ref[:, cs]
        inner = g - jnp.mean(g, axis=1, keepdims=True)
        inner = inner - hat * jnp.mean(g * hat, axis=1, keepdims=True)
        dst[:, cs] = (inv_ref[:, cs] * inner).astype(BF16)

    def backward(hp):
        for j in range(2):
            cs = block(2 * hp + j, hd)
            d = full[0, cs, :].astype(BF16)
            back(mm(values[:, cs], d, NT), gain_k, khat, kinv, dk, cs)
            back(mm(keys[:, cs], d, NN), gain_v, vhat, vinv, dv, cs)

    def tail(i):
        rs = slice(i * pair, (i + 1) * pair)
        acc[:, rs] = mm(dk[...], wk[rs, :], NT) + mm(dv[...], wv[rs, :], NT)

    for hp in own_pairs:
        backward(hp)
    arrive(qdy)
    for hp in peer_pairs:
        backward(hp)
    for i in range(npair):
        tail(i)

    def dquery(hp):
        for j in range(2):
            cs = block(2 * hp + j, hd)
            g = full[1, cs, :].astype(BF16)
            dq[:, cs] = jnp.where(live(hd), mm(cot[:, cs], g, NT), 0.0).astype(BF16)

    kv = core_gather(1, kv)
    for hp in own_pairs:
        dquery(hp)
    cs = block(core, width // 2)
    for i in range(npair):
        rs = slice(i * pair, (i + 1) * pair)
        acc[:, rs] += mm(dq[:, cs], wq[rs, cs], NT)
    arrive(kv)
    for hp in peer_pairs:
        dquery(hp)
    cs = block(1 - core, width // 2)
    for i in range(npair):
        rs = slice(i * pair, (i + 1) * pair)
        out[:, rs] = (acc[:, rs] + mm(dq[:, cs], wq[rs, cs], NT)).astype(BF16)
    for c in sent:
        c.wait_send()


def body(n, points, cotangent, counts, w_query, w_key, w_value, gain_key, bias_key, gain_value, bias_value):
    rows, width = points.shape
    hd = width // HEADS
    grows = HEADS * hd
    chips = n // 2
    piece = grows // n
    ncopies = 3 * chips
    anyspec = pl.BlockSpec(memory_space=pl.ANY)
    vspec = pl.BlockSpec(memory_space=pltpu.VMEM)

    def v(shape, dtype):
        return pltpu.VMEM(shape, dtype)

    return pl.pallas_call(
        functools.partial(kernel, n),
        out_shape=jax.ShapeDtypeStruct((rows, width), BF16),
        in_specs=[pl.BlockSpec(memory_space=pltpu.SMEM)] + [anyspec] * 5 + [pl.BlockSpec(memory_space=pltpu.HBM)] * 4,
        out_specs=vspec,
        scratch_shapes=[
            v((rows, width), BF16),
            v((rows, width), BF16),
            v((width, width), BF16),
            v((width, width), BF16),
            v((width, width), BF16),
            v((rows, width), F32),
            v((rows, width), F32),
            v((rows, width), F32),
            v((rows, width), F32),
            v((rows, width), BF16),
            v((rows, width), BF16),
            v((rows, width), BF16),
            v((rows, width), BF16),
            v((rows, width), BF16),
            v((1, width), F32),
            v((1, width), F32),
            v((1, width), F32),
            v((1, width), F32),
            v((rows, width), F32),
            v((2, grows, hd), F32),
            v((2, grows // 2, hd), F32),
            v((2, chips, piece + 8, hd), F32),
            v((2, chips, piece + 8, hd), F32),
            v((2, grows, hd), F32),
            v((3, 8, hd), F32),
            pltpu.SemaphoreType.DMA((9,)),
            pltpu.SemaphoreType.DMA((2, ncopies)),
            pltpu.SemaphoreType.DMA((2, ncopies)),
            pltpu.SemaphoreType.DMA((1,)),
            pltpu.SemaphoreType.DMA((1,)),
        ],
        compiler_params=pltpu.CompilerParams(
            collective_id=0, has_side_effects=True, vmem_limit_bytes=63 * 2**20
        ),
        cost_estimate=pl.CostEstimate(
            flops=12 * rows * width * width, bytes_accessed=12 * 2**20, transcendentals=0
        ),
    )(
        counts,
        points,
        cotangent,
        w_query,
        w_key,
        w_value,
        gain_key.reshape(1, -1),
        bias_key.reshape(1, -1),
        gain_value.reshape(1, -1),
        bias_value.reshape(1, -1),
    )


def solution(mesh):
    split = P(("group", "dx"), None)
    placed = (split, split, P(("group", "dx")), P(), P(), P(), P(), P(), P(), P())
    return jax.shard_map(
        functools.partial(body, mesh.shape["dx"]),
        mesh=mesh,
        in_specs=placed,
        out_specs=split,
        check_vma=False,
    )
```
